32 devices in a mesh: super: 8 (over z, x), col: 4 (over y, core).
Axes of the slice: x: 2, y: 2, z: 4, core: 2. Of those that a mesh axis runs over, the one named last changes fastest.
Arguments:
- parent: int32 [32, 4], P('super'), may hold values from 0 to 7, as said below
- off_blocks: bfloat16 [32, 4, 512, 512], P('super', None, 'col'), may hold values from -0.25 to 0.25
- inv_factors: bfloat16 [32, 512, 512], P('super', 'col'), as said below
- arrow_rows: bfloat16 [32, 64, 512], P('super'), may hold values from -0.046875 to 0.046875
- target_blocks: float32 [8, 512, 512], P('super'), as said below
- arrow_block: float32 [64, 64], replicated, may hold values from -6 to 6
Outputs:
- factor_blocks: float32 [8, 512, 512], P('super', 'col')
- arrow_update: float32 [64, 64], replicated
The draws below stay inside these ranges and needn't reach their ends.
Inputs may be any that keep to these rules, and one draw needn't show every extreme that they name: Each eliminated supernode names 4 different parents; among the 16 entries of one index of super at most 2 name the same parent. `inv_factors`: each block is lower triangular. `target_blocks`: each block is symmetric, and stays positive definite after the Schur sums of its children are subtracted.
All inputs are finite; a program needn't handle non-finite values.
Results may differ from the reference program's by a relative error of at most 0.00115.
Values may be sent and summed in bfloat16 or wider, within the bound.
A program may use at most 128 MiB of HBM per device.

```python
import jax
import jax.numpy as jnp
from jax import lax

B = 512
ARROW = 64
TARGETS = 4
SN_DEV = 4
SRC = 32
TGT = 8
MOST = 2
N_SUPER = 8


def parent_table(key):
    base_key = jax.random.fold_in(key, 101)
    item_count = SN_DEV * TARGETS
    slot_total = TGT * MOST
    level_count = max(1, min(TGT, item_count).bit_length())
    exponent = jax.random.randint(jax.random.fold_in(base_key, 3), (), 0, level_count)
    popular_count = jnp.minimum(jnp.left_shift(jnp.int32(1), exponent.astype(jnp.int32)), min(TGT, item_count))
    shuffled = jax.random.permutation(jax.random.fold_in(base_key, 1), TGT)
    rank = jnp.zeros((TGT,), jnp.int32).at[shuffled].set(jnp.arange(TGT, dtype=jnp.int32))
    popular = rank < popular_count
    leading = rank == 0
    slot_index = jnp.arange(slot_total, dtype=jnp.int32)
    slot_target = slot_index // MOST
    slot_order = slot_index % MOST

    def one_device(device):
        device_key = jax.random.fold_in(base_key, device + 2)
        jitter = jax.random.randint(jax.random.fold_in(device_key, 0), (slot_total,), 0, 4096)
        second = jax.random.randint(jax.random.fold_in(device_key, 3), (TGT,), 0, 2)
        tier = jnp.where(leading[slot_target], 3, jnp.where(popular[slot_target], jnp.where(slot_order == 0, 2, second[slot_target]), 0))
        scores = tier.astype(jnp.int32) * (1 << 28) + jitter * slot_total + slot_index
        chosen = lax.top_k(scores, item_count)[1]
        ordered = jnp.sort(chosen)
        targets = slot_target[ordered]
        table = targets.reshape(TARGETS, SN_DEV).T
        reorder = jax.random.permutation(jax.random.fold_in(device_key, 1), SN_DEV)
        column_order = jax.random.permutation(jax.random.fold_in(device_key, 2), TARGETS)
        return table[reorder][:, column_order]
    return jax.vmap(one_device)(jnp.arange(N_SUPER, dtype=jnp.int32)).reshape(SRC, TARGETS).astype(jnp.int32)


def draw_parent(key, part):
    return parent_table(key)


def draw_inv_factors(key, part):
    base_key = jax.random.fold_in(key, 404)
    rows = jnp.arange(B, dtype=jnp.int32)[:, None]
    cols = jnp.arange(B, dtype=jnp.int32)[None, :]
    strict = (cols < rows).astype(jnp.float32)
    identity = (cols == rows).astype(jnp.float32)
    lower_part = jax.random.truncated_normal(jax.random.fold_in(base_key, 1), -4.0, 4.0, (SRC, B, B), jnp.float32)
    diagonal = jax.random.uniform(jax.random.fold_in(base_key, 2), (SRC, B, 1), jnp.float32, 0.8, 1.2)
    values = lower_part * B ** (-0.5) * strict + diagonal * identity
    return values.astype(jnp.bfloat16)


def draw_target_blocks(key, part):
    parents = parent_table(key).reshape(SRC * TARGETS)
    counts = jnp.sum((parents[None, :] == jnp.arange(TGT, dtype=jnp.int32)[:, None]).astype(jnp.float32), axis=1)
    level = 2.0 * counts + 12.0 * jnp.sqrt(counts) + 12.0
    base_key = jax.random.fold_in(key, 505)
    raw = jax.random.truncated_normal(base_key, -4.0, 4.0, (TGT, B, B), jnp.float32)
    decay = jax.random.uniform(jax.random.fold_in(base_key, 7), (TGT, 1, 1), jnp.float32, 0.75, 0.85)
    symmetric = (raw + jnp.swapaxes(raw, 1, 2)) * (0.5 * B ** (-0.5) / 1.4142135)
    row_ids = jnp.arange(B, dtype=jnp.int32)[:, None]
    col_ids = jnp.arange(B, dtype=jnp.int32)[None, :]
    identity = (row_ids == col_ids).astype(jnp.float32)
    distance = jnp.abs(row_ids - col_ids).astype(jnp.float32)
    kernel = jnp.exp(distance[None, :, :] * jnp.log(decay))
    sign_draw = jax.random.bernoulli(jax.random.fold_in(base_key, 8), 0.5, (TGT, B))
    magnitude = jax.random.uniform(jax.random.fold_in(base_key, 9), (TGT, B), jnp.float32, 0.8, 1.25)
    scaling = jnp.where(sign_draw, 1.0, -1.0).astype(jnp.float32) * magnitude
    dense = scaling[:, :, None] * kernel * scaling[:, None, :]
    return symmetric + level[:, None, None] * (identity[None, :, :] + dense)


def shard_levels(stream_key, shape, pieces, least, largest):
    level = 1.0
    for dim, parts in pieces:
        draws = jax.random.uniform(jax.random.fold_in(jax.random.fold_in(stream_key, 6), dim), (parts,), jnp.float32, least / len(pieces), largest / len(pieces))
        level = level * jnp.repeat(jnp.exp(draws), shape[dim] // parts).reshape((-1,) + (1,) * (len(shape) - 1 - dim))
    return level


def gaussian(rng, shape, scale, bound, cuts=(), kind=jnp.bfloat16):
    array = scale * jax.random.normal(rng, shape, jnp.float32)
    if cuts:
        array = array * shard_levels(rng, shape, cuts, -0.22, 0.18)
    return jnp.clip(array, -bound, bound).astype(kind)


def setup_inputs(seed: int = 0) -> dict:
    streams_of = jax.random.split(jax.random.key(seed), 7)
    parent = draw_parent(jax.random.fold_in(streams_of[6], 71), 0)
    off_blocks = gaussian(streams_of[1], (SRC, TARGETS, B, B), B ** -0.5, 0.25, ((0, 8), (2, 4)))
    inv_factors = draw_inv_factors(jax.random.fold_in(streams_of[6], 71), 0)
    arrow_rows = gaussian(streams_of[3], (SRC, ARROW, B), (B * SRC) ** -0.5, 0.046875, ((0, 8),))
    target_blocks = draw_target_blocks(jax.random.fold_in(streams_of[6], 71), 0)
    arrow_block = gaussian(streams_of[5], (ARROW, ARROW), 1.0, 6.0, (), jnp.float32)
    return dict(parent=parent, off_blocks=off_blocks, inv_factors=inv_factors, arrow_rows=arrow_rows, target_blocks=target_blocks, arrow_block=arrow_block)


def reference(parent, off_blocks, inv_factors, arrow_rows, target_blocks, arrow_block):

    def one_source(running, inputs):
        schur_sum, arrow_sum = running
        parent_ids, off_part, inverse, arrow_part = inputs
        outer_list = []
        for target_index in range(TARGETS):
            panel_cols = jnp.dot(off_part[target_index].astype(jnp.float32), inverse.T.astype(jnp.float32), preferred_element_type=jnp.float32).astype(jnp.bfloat16)
            outer_list.append(jnp.dot(panel_cols.astype(jnp.float32), panel_cols.T.astype(jnp.float32), preferred_element_type=jnp.float32))
        schur_sum = schur_sum.at[parent_ids].add(jnp.stack(outer_list))
        arrow_panel = jnp.dot(arrow_part.astype(jnp.float32), inverse.T.astype(jnp.float32), preferred_element_type=jnp.float32).astype(jnp.bfloat16)
        arrow_sum = arrow_sum + jnp.dot(arrow_panel.astype(jnp.float32), arrow_panel.T.astype(jnp.float32), preferred_element_type=jnp.float32)
        return ((schur_sum, arrow_sum), None)
    initial = (jnp.zeros((TGT, B, B), jnp.float32), jnp.zeros((ARROW, ARROW), jnp.float32))
    results, unused = lax.scan(one_source, initial, (parent.astype(jnp.int32), off_blocks, inv_factors, arrow_rows))
    schur_sum, arrow_sum = results
    updated = target_blocks - schur_sum
    factors = lax.map(jnp.linalg.cholesky, updated)
    return (factors, arrow_block - arrow_sum)
```

```python
import functools

import jax
import jax.numpy as jnp
from jax import lax
from jax.experimental import pallas as pl
from jax.experimental.pallas import tpu as pltpu
from jax.sharding import PartitionSpec as P

MESH = pl.DeviceIdType.MESH
EXACT = lax.Precision.HIGHEST
BLK = 128
SUB = 8


def block_pairs(blocks):
    return [(r, c) for r in range(blocks) for c in range(r, blocks)]


def eliminate(rows, extra, step):
    row_ids = lax.broadcasted_iota(jnp.int32, (SUB, BLK), 0)
    base = step * SUB
    cols = [
        jnp.broadcast_to(rows[:, base + b : base + b + 1], (SUB, BLK)) for b in range(SUB)
    ]
    scale = jnp.zeros((SUB, BLK), jnp.float32)
    for m in range(SUB):
        pivot = jnp.broadcast_to(cols[m][m : m + 1], (SUB, BLK))
        inv = lax.rsqrt(pivot)
        scale = jnp.where(row_ids == m, inv, scale)
        if m == SUB - 1:
            break
        low = cols[m] * inv
        for b in range(m + 1, SUB):
            cols[b] = cols[b] - low * jnp.broadcast_to(low[b : b + 1], (SUB, BLK))
        low = jnp.where(row_ids > m, low * inv, 0.0)
        rows = rows - low * jnp.broadcast_to(rows[m : m + 1], (SUB, BLK))
        if extra is not None:
            extra = extra - low * jnp.broadcast_to(extra[m : m + 1], (SUB, BLK))
    return rows * scale, None if extra is None else extra * scale


def cholesky_kernel(target_ref, total_ref, out_ref, u_ref, d_ref, q_ref):
    blocks = target_ref.shape[1] // BLK
    pairs = block_pairs(blocks)
    row_ids = lax.broadcasted_iota(jnp.int32, (BLK, BLK), 0)
    col_ids = lax.broadcasted_iota(jnp.int32, (BLK, BLK), 1)
    for kb in range(blocks):
        lo = kb * BLK
        update = None
        if kb:
            update = lax.dot_general(
                u_ref[0:lo, lo : lo + BLK],
                u_ref[0:lo, lo:],
                (((0,), (0,)), ((), ())),
                precision=EXACT,
                preferred_element_type=jnp.float32,
            )
        panel = []
        for cb in range(kb, blocks):
            part = target_ref[0, lo : lo + BLK, cb * BLK : (cb + 1) * BLK]
            part = part - total_ref[pairs.index((kb, cb))].astype(jnp.float32)
            if kb:
                part = part - update[:, (cb - kb) * BLK : (cb - kb + 1) * BLK]
            panel.append(part)
        last = kb == blocks - 1
        d_ref[...] = panel[0]
        if not last:
            q_ref[...] = (row_ids == col_ids).astype(jnp.float32)
        steps = BLK // SUB
        for step in range(steps):
            here = slice(step * SUB, (step + 1) * SUB)
            rows, extra = eliminate(d_ref[here], None if last else q_ref[here], step)
            d_ref[here] = rows
            if not last:
                q_ref[here] = extra
            if step < steps - 1:
                below = slice((step + 1) * SUB, BLK)
                right = rows if last else jnp.concatenate([rows, extra], axis=1)
                change = lax.dot_general(
                    rows,
                    right,
                    (((0,), (0,)), ((), ())),
                    precision=EXACT,
                    preferred_element_type=jnp.float32,
                )
                d_ref[below] = d_ref[below] - change[below, :BLK]
                if not last:
                    q_ref[below] = q_ref[below] - change[below, BLK:]
        u_ref[lo : lo + BLK, lo : lo + BLK] = jnp.where(row_ids <= col_ids, d_ref[...], 0.0)
        if not last:
            u_ref[lo : lo + BLK, lo + BLK :] = jnp.dot(
                q_ref[...],
                jnp.concatenate(panel[1:], axis=1),
                precision=EXACT,
                preferred_element_type=jnp.float32,
            )
    me = lax.axis_index("col")
    for mine in range(blocks):

        @pl.when(me == mine)
        def _():
            for b in range(blocks):
                there = slice(b * BLK, (b + 1) * BLK)
                if b <= mine:
                    out_ref[0, :, there] = u_ref[there, mine * BLK : (mine + 1) * BLK].T
                else:
                    out_ref[0, :, there] = jnp.zeros((BLK, BLK), jnp.float32)


def factor_rows(target_blocks, total):
    width = target_blocks.shape[1]
    vmem = pl.BlockSpec(memory_space=pltpu.VMEM)
    return pl.pallas_call(
        cholesky_kernel,
        out_shape=jax.ShapeDtypeStruct((1, BLK, width), jnp.float32),
        in_specs=[vmem, vmem],
        out_specs=vmem,
        scratch_shapes=[
            pltpu.VMEM((width, width), jnp.float32),
            pltpu.VMEM((BLK, BLK), jnp.float32),
            pltpu.VMEM((BLK, BLK), jnp.float32),
        ],
        compiler_params=pltpu.CompilerParams(vmem_limit_bytes=24 * 2**20),
        name="factor",
    )(target_blocks, total)

def routed(parent, off_blocks, inv_factors, arrow_rows):
    supers = lax.axis_size("super")
    sources, fanout, slab_rows, block_width = off_blocks.shape
    item_count = sources * fanout
    capacity = max(2, (item_count + supers - 1) // supers)
    stacked_rows = off_blocks.reshape(sources, fanout * slab_rows, block_width)
    portion = lax.all_gather(inv_factors, "col", axis=1, tiled=True)
    rows_part = jnp.einsum(
        "jrk,jck->jrc", stacked_rows, portion, preferred_element_type=jnp.float32
    ).astype(jnp.bfloat16)
    arrow_panels = jnp.einsum(
        "jak,jck->jac", arrow_rows, portion, preferred_element_type=jnp.float32
    ).astype(jnp.bfloat16)
    arrow_local = jnp.einsum(
        "jac,jbc->ab", arrow_panels, arrow_panels, preferred_element_type=jnp.float32
    )
    arrow_total = lax.psum(arrow_local, "super")
    row_panels = rows_part.reshape(sources, fanout, slab_rows, block_width)
    panels = lax.all_to_all(row_panels, "col", split_axis=3, concat_axis=2, tiled=True)
    column_panels = panels.reshape(item_count, block_width, panels.shape[3])
    owners = parent.reshape(item_count)
    item_index = jnp.arange(item_count, dtype=jnp.int32)
    matching = owners[:, None] == owners[None, :]
    earlier = item_index[None, :] < item_index[:, None]
    position = jnp.sum((matching & earlier).astype(jnp.int32), axis=1)
    target_slot = owners * capacity + position
    slots = jnp.arange(supers * capacity, dtype=jnp.int32)
    chosen = (slots[:, None] == target_slot[None, :]).astype(jnp.bfloat16)
    packed = jnp.einsum(
        "pi,irc->prc", chosen, column_panels, preferred_element_type=jnp.float32
    ).astype(jnp.bfloat16)
    packed = packed.reshape(supers, capacity, block_width, column_panels.shape[2])
    received = lax.all_to_all(packed, "super", split_axis=0, concat_axis=0, tiled=True)
    schur_local = jnp.einsum(
        "dmrc,dmsc->rs", received, received, preferred_element_type=jnp.float32
    )
    schur = lax.psum(schur_local.astype(jnp.bfloat16), "col")
    blocks = block_width // BLK
    total = jnp.stack(
        [
            schur[r * BLK : (r + 1) * BLK, c * BLK : (c + 1) * BLK]
            for r, c in block_pairs(blocks)
        ]
    )
    return total, arrow_total


def shards(parent, off_blocks, inv_factors, arrow_rows, target_blocks, arrow_block):
    total, arrow_total = routed(parent, off_blocks, inv_factors, arrow_rows)
    return factor_rows(target_blocks, total), arrow_block - arrow_total


def solution(mesh):
    placed = (
        P("super", None),
        P("super", None, "col", None),
        P("super", "col", None),
        P("super", None, None),
        P("super", None, None),
        P(),
    )
    return jax.shard_map(
        shards,
        mesh=mesh,
        in_specs=placed,
        out_specs=(P("super", "col", None), P()),
        check_vma=False,
    )
```

```python
import functools

import jax
import jax.numpy as jnp
from jax import lax
from jax.experimental import pallas as pl
from jax.experimental.pallas import tpu as pltpu
from jax.sharding import PartitionSpec as P

MESH = pl.DeviceIdType.MESH
EXACT = lax.Precision.HIGHEST
BLK = 128
SUB = 8


def block_pairs(blocks):
    return [(r, c) for r in range(blocks) for c in range(r, blocks)]


def eliminate(rows, extra, step):
    row_ids = lax.broadcasted_iota(jnp.int32, (SUB, BLK), 0)
    base = step * SUB
    cols = [
        jnp.broadcast_to(rows[:, base + b : base + b + 1], (SUB, BLK)) for b in range(SUB)
    ]
    scale = jnp.zeros((SUB, BLK), jnp.float32)
    for m in range(SUB):
        pivot = jnp.broadcast_to(cols[m][m : m + 1], (SUB, BLK))
        inv = lax.rsqrt(pivot)
        scale = jnp.where(row_ids == m, inv, scale)
        if m == SUB - 1:
            break
        low = cols[m] * inv
        for b in range(m + 1, SUB):
            cols[b] = cols[b] - low * jnp.broadcast_to(low[b : b + 1], (SUB, BLK))
        low = jnp.where(row_ids > m, low * inv, 0.0)
        rows = rows - low * jnp.broadcast_to(rows[m : m + 1], (SUB, BLK))
        if extra is not None:
            extra = extra - low * jnp.broadcast_to(extra[m : m + 1], (SUB, BLK))
    return rows * scale, None if extra is None else extra * scale


def cholesky_kernel(target_ref, total_ref, out_ref, u_ref, d_ref, q_ref):
    blocks = target_ref.shape[1] // BLK
    pairs = block_pairs(blocks)
    row_ids = lax.broadcasted_iota(jnp.int32, (BLK, BLK), 0)
    col_ids = lax.broadcasted_iota(jnp.int32, (BLK, BLK), 1)
    for kb in range(blocks):
        lo = kb * BLK
        update = None
        if kb:
            update = lax.dot_general(
                u_ref[0:lo, lo : lo + BLK],
                u_ref[0:lo, lo:],
                (((0,), (0,)), ((), ())),
                precision=EXACT,
                preferred_element_type=jnp.float32,
            )
        panel = []
        for cb in range(kb, blocks):
            part = target_ref[0, lo : lo + BLK, cb * BLK : (cb + 1) * BLK]
            part = part - total_ref[pairs.index((kb, cb))].astype(jnp.float32)
            if kb:
                part = part - update[:, (cb - kb) * BLK : (cb - kb + 1) * BLK]
            panel.append(part)
        last = kb == blocks - 1
        d_ref[...] = panel[0]
        if not last:
            q_ref[...] = (row_ids == col_ids).astype(jnp.float32)
        steps = BLK // SUB
        for step in range(steps):
            here = slice(step * SUB, (step + 1) * SUB)
            rows, extra = eliminate(d_ref[here], None if last else q_ref[here], step)
            d_ref[here] = rows
            if not last:
                q_ref[here] = extra
            if step < steps - 1:
                below = slice((step + 1) * SUB, BLK)
                right = rows if last else jnp.concatenate([rows, extra], axis=1)
                change = lax.dot_general(
                    rows,
                    right,
                    (((0,), (0,)), ((), ())),
                    precision=EXACT,
                    preferred_element_type=jnp.float32,
                )
                d_ref[below] = d_ref[below] - change[below, :BLK]
                if not last:
                    q_ref[below] = q_ref[below] - change[below, BLK:]
        u_ref[lo : lo + BLK, lo : lo + BLK] = jnp.where(row_ids <= col_ids, d_ref[...], 0.0)
        if not last:
            u_ref[lo : lo + BLK, lo + BLK :] = jnp.dot(
                q_ref[...],
                jnp.concatenate(panel[1:], axis=1),
                precision=EXACT,
                preferred_element_type=jnp.float32,
            )
    me = lax.axis_index("col")
    for mine in range(blocks):

        @pl.when(me == mine)
        def _():
            for b in range(blocks):
                there = slice(b * BLK, (b + 1) * BLK)
                if b <= mine:
                    out_ref[0, :, there] = u_ref[there, mine * BLK : (mine + 1) * BLK].T
                else:
                    out_ref[0, :, there] = jnp.zeros((BLK, BLK), jnp.float32)


def factor_rows(target_blocks, total):
    width = target_blocks.shape[1]
    vmem = pl.BlockSpec(memory_space=pltpu.VMEM)
    return pl.pallas_call(
        cholesky_kernel,
        out_shape=jax.ShapeDtypeStruct((1, BLK, width), jnp.float32),
        in_specs=[vmem, vmem],
        out_specs=vmem,
        scratch_shapes=[
            pltpu.VMEM((width, width), jnp.float32),
            pltpu.VMEM((BLK, BLK), jnp.float32),
            pltpu.VMEM((BLK, BLK), jnp.float32),
        ],
        compiler_params=pltpu.CompilerParams(vmem_limit_bytes=24 * 2**20),
        name="factor",
    )(target_blocks, total)

def routed(parent, off_blocks, inv_factors, arrow_rows):
    supers = lax.axis_size("super")
    sources, fanout, slab_rows, block_width = off_blocks.shape
    item_count = sources * fanout
    capacity = max(2, (item_count + supers - 1) // supers)
    stacked_rows = off_blocks.reshape(sources, fanout * slab_rows, block_width)
    portion = lax.all_gather(inv_factors, "col", axis=1, tiled=True)
    rows_part = jnp.einsum(
        "jrk,jck->jrc", stacked_rows, portion, preferred_element_type=jnp.float32
    ).astype(jnp.bfloat16)
    arrow_panels = jnp.einsum(
        "jak,jck->jac", arrow_rows, portion, preferred_element_type=jnp.float32
    ).astype(jnp.bfloat16)
    arrow_local = jnp.einsum(
        "jac,jbc->ab", arrow_panels, arrow_panels, preferred_element_type=jnp.float32
    )
    arrow_total = lax.psum(arrow_local, "super")
    row_panels = rows_part.reshape(sources, fanout, slab_rows, block_width)
    panels = lax.all_to_all(row_panels, "col", split_axis=3, concat_axis=2, tiled=True)
    column_panels = panels.reshape(item_count, block_width, panels.shape[3])
    owners = parent.reshape(item_count)
    item_index = jnp.arange(item_count, dtype=jnp.int32)
    matching = owners[:, None] == owners[None, :]
    earlier = item_index[None, :] < item_index[:, None]
    position = jnp.sum((matching & earlier).astype(jnp.int32), axis=1)
    target_slot = owners * capacity + position
    slots = jnp.arange(supers * capacity, dtype=jnp.int32)
    chosen = (slots[:, None] == target_slot[None, :]).astype(jnp.bfloat16)
    packed = jnp.einsum(
        "pi,irc->prc", chosen, column_panels, preferred_element_type=jnp.float32
    ).astype(jnp.bfloat16)
    packed = packed.reshape(supers, capacity, block_width, column_panels.shape[2])
    received = lax.all_to_all(packed, "super", split_axis=0, concat_axis=0, tiled=True)
    schur_local = jnp.einsum(
        "dmrc,dmsc->rs", received, received, preferred_element_type=jnp.float32
    )
    schur = lax.psum(schur_local.astype(jnp.bfloat16), "col")
    blocks = block_width // BLK
    total = jnp.stack(
        [
            schur[r * BLK : (r + 1) * BLK, c * BLK : (c + 1) * BLK]
            for r, c in block_pairs(blocks)
        ]
    )
    return total, arrow_total


def exchange_kernel(
    supers, cols, fanout,
    parent_ref, off_ref, inv_ref, arrow_rows_ref, arrow_block_ref,
    total_ref, arrow_ref,
    inv_all, outgoing, off_all, panel, sums, landed, arrow_all, total,
    inv_send, inv_recv, off_send, off_recv, sum_send, sum_recv,
    arrow_send, arrow_recv, cast_send, cast_recv,
):
    sources = inv_ref.shape[0]
    slab = inv_ref.shape[1]
    width = inv_ref.shape[2]
    blocks = width // BLK
    pairs = block_pairs(blocks)
    rounds = supers // cols
    me_s, me_c = lax.axis_index("super"), lax.axis_index("col")
    y, core = lax.div(me_c, 2), lax.rem(me_c, 2)
    beside = 2 * y + 1 - core
    across = 2 * (1 - y) + core
    diagonal = 2 * (1 - y) + 1 - core
    peers = (beside, across, diagonal)

    barrier = pltpu.get_barrier_semaphore()
    for peer in peers:
        pl.semaphore_signal(
            barrier, inc=1, device_id={"super": me_s, "col": peer}, device_id_type=MESH
        )
    for d in range(1, supers):
        pl.semaphore_signal(
            barrier,
            inc=1,
            device_id={"super": lax.rem(me_s + d, supers), "col": me_c},
            device_id_type=MESH,
        )
    pl.semaphore_wait(barrier, cols - 1 + supers - 1)

    def remote(src, dst, send, recv, sup, col):
        return pltpu.make_async_remote_copy(
            src_ref=src,
            dst_ref=dst,
            send_sem=send,
            recv_sem=recv,
            device_id={"super": sup, "col": col},
            device_id_type=MESH,
        )

    inv_across = remote(inv_ref, inv_all.at[:, me_c], inv_send.at[1], inv_recv.at[1], me_s, across)
    inv_across.start()
    inv_beside = remote(inv_ref, inv_all.at[:, me_c], inv_send.at[0], inv_recv.at[0], me_s, beside)
    inv_beside.start()

    entries = [
        (parent_ref[j, t], j * fanout + t, j) for j in range(sources) for t in range(fanout)
    ]
    half = lax.div(me_s, cols)

    def parent_of(col, t):
        return col + cols * lax.rem(half + 1 + t, rounds)

    def items(col, t):
        p = parent_of(col, t)
        first, first_source = jnp.int32(len(entries) - 1), jnp.int32(sources - 1)
        second, second_source = jnp.int32(0), jnp.int32(0)
        for owner, item, source in entries:
            hit = owner == p
            first = jnp.where(hit, jnp.minimum(first, item), first)
            first_source = jnp.where(hit, jnp.minimum(first_source, source), first_source)
            second = jnp.where(hit, item, second)
            second_source = jnp.where(hit, source, second_source)
        return (first, second), (first_source, second_source)

    off_copies = {}
    own_sources = []
    for t in range(rounds):
        for k in (1, 2, 0):
            chosen, _ = items(peers[k], t)
            for m in range(2):
                outgoing[k, t, m] = off_ref[chosen[m]]
            copy = remote(
                outgoing.at[k, t],
                off_all.at[t, :, me_c],
                off_send.at[k, t],
                off_recv.at[k, t],
                me_s,
                peers[k],
            )
            copy.start()
            off_copies[k, t] = copy
        chosen, chosen_sources = items(me_c, t)
        own_sources.append(chosen_sources)
        for m in range(2):
            off_all[t, m, me_c] = off_ref[chosen[m]]
    for j in range(sources):
        inv_all[j, me_c] = inv_ref[j]

    inv_across.wait_recv()
    inv_onward = remote(
        inv_all.at[:, across], inv_all.at[:, across], inv_send.at[2], inv_recv.at[2], me_s, beside
    )
    inv_onward.start()
    inv_beside.wait_recv()
    inv_onward.wait_recv()

    nt = (((1,), (1,)), ((), ()))
    arrow_sum = jnp.zeros(arrow_ref.shape, jnp.float32)
    for j in range(sources):
        rows = lax.dot_general(
            arrow_rows_ref[j],
            inv_all[j].reshape(width, width),
            nt,
            preferred_element_type=jnp.float32,
        ).astype(jnp.bfloat16)
        arrow_sum = arrow_sum + lax.dot_general(
            rows, rows, nt, preferred_element_type=jnp.float32
        )
    arrow_all[me_s] = arrow_sum
    arrow_copies = []
    for d in range(1, supers):
        copy = remote(
            arrow_all.at[me_s],
            arrow_all.at[me_s],
            arrow_send.at[d],
            arrow_recv.at[d],
            lax.rem(me_s + d, supers),
            me_c,
        )
        copy.start()
        arrow_copies.append(copy)

    for t in range(rounds):
        for k in range(3):
            off_copies[k, t].wait_recv()
        for m in range(2):
            panel[:, m * width : (m + 1) * width] = lax.dot_general(
                off_all[t, m].reshape(width, width),
                inv_all[own_sources[t][m]].reshape(width, width),
                nt,
                preferred_element_type=jnp.float32,
            ).astype(jnp.bfloat16)
        for r in range(blocks):
            product = lax.dot_general(
                panel[r * BLK : (r + 1) * BLK, :],
                panel[r * BLK :, :],
                nt,
                preferred_element_type=jnp.float32,
            ).astype(jnp.bfloat16)
            for c in range(r, blocks):
                sums[t, pairs.index((r, c))] = product[:, (c - r) * BLK : (c - r + 1) * BLK]
        p = parent_of(me_c, t)

        @pl.when(p != me_s)
        def _():
            remote(
                sums.at[t], landed.at[me_s], sum_send.at[t], sum_recv.at[me_s], p, me_c
            ).start()

        @pl.when(p == me_s)
        def _():
            landed[me_s] = sums[t]

    chief = lax.rem(me_s, cols)

    def cast(n, col):
        return remote(total, total, cast_send.at[n], cast_recv.at[0], me_s, col)

    @pl.when(me_c == chief)
    def _():
        for d in range(1, supers):
            s = lax.rem(me_s + d, supers)
            remote(
                sums.at[0], landed.at[s], sum_send.at[0], sum_recv.at[s], me_s, beside
            ).wait_recv()
        for b in range(len(pairs)):
            acc = landed[0, b].astype(jnp.float32)
            for s in range(1, supers):
                acc = acc + landed[s, b].astype(jnp.float32)
            total[b] = acc.astype(jnp.bfloat16)
        first, second = cast(0, across), cast(1, beside)
        first.start()
        second.start()
        first.wait_send()
        second.wait_send()

    @pl.when(me_c != chief)
    def _():
        cast(0, beside).wait_recv()

    @pl.when(across == chief)
    def _():
        onward = cast(1, beside)
        onward.start()
        onward.wait_send()

    total_ref[...] = total[...]

    for copy in arrow_copies:
        copy.wait_recv()
    arrow_total = arrow_all[0]
    for s in range(1, supers):
        arrow_total = arrow_total + arrow_all[s]
    arrow_ref[...] = arrow_block_ref[...] - arrow_total

    for copy in (inv_across, inv_beside, inv_onward, *off_copies.values(), *arrow_copies):
        copy.wait_send()
    for t in range(rounds):
        p = parent_of(me_c, t)

        @pl.when(p != me_s)
        def _():
            remote(
                sums.at[t], landed.at[me_s], sum_send.at[t], sum_recv.at[me_s], p, me_c
            ).wait_send()


def exchanged(parent, off_blocks, inv_factors, arrow_rows, arrow_block):
    supers, cols = lax.axis_size("super"), lax.axis_size("col")
    sources, fanout, slab, width = off_blocks.shape
    arrow = arrow_block.shape[0]
    rounds = supers // cols
    count = len(block_pairs(width // BLK))
    vmem = pl.BlockSpec(memory_space=pltpu.VMEM)
    bf16, f32 = jnp.bfloat16, jnp.float32
    dma = pltpu.SemaphoreType.DMA
    return pl.pallas_call(
        functools.partial(exchange_kernel, supers, cols, fanout),
        out_shape=(
            jax.ShapeDtypeStruct((count, BLK, BLK), bf16),
            jax.ShapeDtypeStruct((arrow, arrow), f32),
        ),
        in_specs=[pl.BlockSpec(memory_space=pltpu.SMEM)] + [vmem] * 4,
        out_specs=(vmem, vmem),
        scratch_shapes=[
            pltpu.VMEM((sources, cols, slab, width), bf16),
            pltpu.VMEM((cols - 1, rounds, 2, slab, width), bf16),
            pltpu.VMEM((rounds, 2, cols, slab, width), bf16),
            pltpu.VMEM((width, 2 * width), bf16),
            pltpu.VMEM((rounds, count, BLK, BLK), bf16),
            pltpu.VMEM((supers, count, BLK, BLK), bf16),
            pltpu.VMEM((supers, arrow, arrow), f32),
            pltpu.VMEM((count, BLK, BLK), bf16),
            dma((3,)),
            dma((3,)),
            dma((3, rounds)),
            dma((3, rounds)),
            dma((rounds,)),
            dma((supers,)),
            dma((supers,)),
            dma((supers,)),
            dma((2,)),
            dma((1,)),
        ],
        compiler_params=pltpu.CompilerParams(
            collective_id=0, has_side_effects=True, vmem_limit_bytes=40 * 2**20
        ),
        name="exchange",
    )(parent, off_blocks.reshape(sources * fanout, slab, width), inv_factors, arrow_rows, arrow_block)


def shards(parent, off_blocks, inv_factors, arrow_rows, target_blocks, arrow_block):
    supers, cols = lax.axis_size("super"), lax.axis_size("col")
    entries = off_blocks.shape[0] * off_blocks.shape[1]
    if cols == 4 and supers == 2 * cols and entries == 2 * supers:
        total, arrow_update = exchanged(parent, off_blocks, inv_factors, arrow_rows, arrow_block)
    else:
        total, arrow_total = routed(parent, off_blocks, inv_factors, arrow_rows)
        arrow_update = arrow_block - arrow_total
    return factor_rows(target_blocks, total), arrow_update


def solution(mesh):
    placed = (
        P("super", None),
        P("super", None, "col", None),
        P("super", "col", None),
        P("super", None, None),
        P("super", None, None),
        P(),
    )
    return jax.shard_map(
        shards,
        mesh=mesh,
        in_specs=placed,
        out_specs=(P("super", "col", None), P()),
        check_vma=False,
    )
```

```python
import functools

import jax
import jax.numpy as jnp
from jax import lax
from jax.experimental import pallas as pl
from jax.experimental.pallas import tpu as pltpu
from jax.sharding import PartitionSpec as P

MESH = pl.DeviceIdType.MESH
EXACT = lax.Precision.HIGHEST
BLK = 128
SUB = 16


def block_pairs(blocks):
    return [(r, c) for r in range(blocks) for c in range(r, blocks)]


def halves(x):
    high = x.astype(jnp.bfloat16)
    return high, (x - high.astype(jnp.float32)).astype(jnp.bfloat16)


def thin_product(a, b):
    a_high, a_low = halves(a)
    b_high, b_low = halves(b)
    return lax.dot_general(
        jnp.concatenate([a_high, a_high, a_low], axis=0),
        jnp.concatenate([b_high, b_low, b_high], axis=0),
        (((0,), (0,)), ((), ())),
        preferred_element_type=jnp.float32,
    )


def eliminate(rows, extra, step):
    row_ids = lax.broadcasted_iota(jnp.int32, (SUB, BLK), 0)
    base = step * SUB
    cols = [
        jnp.broadcast_to(rows[:, base + b : base + b + 1], (SUB, BLK)) for b in range(SUB)
    ]
    scale = jnp.zeros((SUB, BLK), jnp.float32)
    for m in range(SUB):
        pivot = jnp.broadcast_to(cols[m][m : m + 1], (SUB, BLK))
        inv = lax.rsqrt(pivot)
        scale = jnp.where(row_ids == m, inv, scale)
        if m == SUB - 1:
            break
        low = cols[m] * inv
        for b in range(m + 1, SUB):
            cols[b] = cols[b] - low * jnp.broadcast_to(low[b : b + 1], (SUB, BLK))
        low = jnp.where(row_ids > m, low * inv, 0.0)
        rows = rows - low * jnp.broadcast_to(rows[m : m + 1], (SUB, BLK))
        if extra is not None:
            extra = extra - low * jnp.broadcast_to(extra[m : m + 1], (SUB, BLK))
    return rows * scale, None if extra is None else extra * scale


def cholesky_kernel(updated_ref, out_ref, u_ref, d_ref, q_ref):
    blocks = out_ref.shape[2] // BLK
    pairs = block_pairs(blocks)
    row_ids = lax.broadcasted_iota(jnp.int32, (BLK, BLK), 0)
    col_ids = lax.broadcasted_iota(jnp.int32, (BLK, BLK), 1)
    for kb in range(blocks):
        lo = kb * BLK
        update = None
        if kb:
            update = lax.dot_general(
                u_ref[0:lo, lo : lo + BLK],
                u_ref[0:lo, lo:],
                (((0,), (0,)), ((), ())),
                precision=EXACT,
                preferred_element_type=jnp.float32,
            )
        panel = []
        for cb in range(kb, blocks):
            part = updated_ref[pairs.index((kb, cb))]
            if kb:
                part = part - update[:, (cb - kb) * BLK : (cb - kb + 1) * BLK]
            panel.append(part)
        last = kb == blocks - 1
        d_ref[...] = panel[0]
        if not last:
            q_ref[...] = (row_ids == col_ids).astype(jnp.float32)
        steps = BLK // SUB
        for step in range(steps):
            here = slice(step * SUB, (step + 1) * SUB)
            rows, extra = eliminate(d_ref[here], None if last else q_ref[here], step)
            d_ref[here] = rows
            if not last:
                q_ref[here] = extra
            if step < steps - 1:
                below = slice((step + 1) * SUB, BLK)
                right = rows if last else jnp.concatenate([rows, extra], axis=1)
                change = thin_product(rows, right)
                d_ref[below] = d_ref[below] - change[below, :BLK]
                if not last:
                    q_ref[below] = q_ref[below] - change[below, BLK:]
        u_ref[lo : lo + BLK, lo : lo + BLK] = jnp.where(row_ids <= col_ids, d_ref[...], 0.0)
        if not last:
            u_ref[lo : lo + BLK, lo + BLK :] = jnp.dot(
                q_ref[...],
                jnp.concatenate(panel[1:], axis=1),
                precision=EXACT,
                preferred_element_type=jnp.float32,
            )
    me = lax.axis_index("col")
    for mine in range(blocks):

        @pl.when(me == mine)
        def _():
            for b in range(blocks):
                there = slice(b * BLK, (b + 1) * BLK)
                if b <= mine:
                    out_ref[0, :, there] = u_ref[there, mine * BLK : (mine + 1) * BLK].T
                else:
                    out_ref[0, :, there] = jnp.zeros((BLK, BLK), jnp.float32)


def factor_rows(updated, width):
    vmem = pl.BlockSpec(memory_space=pltpu.VMEM)
    return pl.pallas_call(
        cholesky_kernel,
        out_shape=jax.ShapeDtypeStruct((1, BLK, width), jnp.float32),
        in_specs=[vmem],
        out_specs=vmem,
        scratch_shapes=[
            pltpu.VMEM((width, width), jnp.float32),
            pltpu.VMEM((BLK, BLK), jnp.float32),
            pltpu.VMEM((BLK, BLK), jnp.float32),
        ],
        compiler_params=pltpu.CompilerParams(vmem_limit_bytes=24 * 2**20),
        name="factor",
    )(updated)

def routed(parent, off_blocks, inv_factors, arrow_rows, target_blocks, arrow_block):
    supers = lax.axis_size("super")
    sources, fanout, slab_rows, block_width = off_blocks.shape
    item_count = sources * fanout
    capacity = max(2, (item_count + supers - 1) // supers)
    stacked_rows = off_blocks.reshape(sources, fanout * slab_rows, block_width)
    portion = lax.all_gather(inv_factors, "col", axis=1, tiled=True)
    rows_part = jnp.einsum(
        "jrk,jck->jrc", stacked_rows, portion, preferred_element_type=jnp.float32
    ).astype(jnp.bfloat16)
    arrow_panels = jnp.einsum(
        "jak,jck->jac", arrow_rows, portion, preferred_element_type=jnp.float32
    ).astype(jnp.bfloat16)
    arrow_local = jnp.einsum(
        "jac,jbc->ab", arrow_panels, arrow_panels, preferred_element_type=jnp.float32
    )
    arrow_total = lax.psum(arrow_local, "super")
    row_panels = rows_part.reshape(sources, fanout, slab_rows, block_width)
    panels = lax.all_to_all(row_panels, "col", split_axis=3, concat_axis=2, tiled=True)
    column_panels = panels.reshape(item_count, block_width, panels.shape[3])
    owners = parent.reshape(item_count)
    item_index = jnp.arange(item_count, dtype=jnp.int32)
    matching = owners[:, None] == owners[None, :]
    earlier = item_index[None, :] < item_index[:, None]
    position = jnp.sum((matching & earlier).astype(jnp.int32), axis=1)
    target_slot = owners * capacity + position
    slots = jnp.arange(supers * capacity, dtype=jnp.int32)
    chosen = (slots[:, None] == target_slot[None, :]).astype(jnp.bfloat16)
    packed = jnp.einsum(
        "pi,irc->prc", chosen, column_panels, preferred_element_type=jnp.float32
    ).astype(jnp.bfloat16)
    packed = packed.reshape(supers, capacity, block_width, column_panels.shape[2])
    received = lax.all_to_all(packed, "super", split_axis=0, concat_axis=0, tiled=True)
    schur_local = jnp.einsum(
        "dmrc,dmsc->rs", received, received, preferred_element_type=jnp.float32
    )
    schur = lax.psum(schur_local.astype(jnp.bfloat16), "col")
    blocks = block_width // BLK
    whole = target_blocks[0] - schur.astype(jnp.float32)
    updated = jnp.stack(
        [
            whole[r * BLK : (r + 1) * BLK, c * BLK : (c + 1) * BLK]
            for r, c in block_pairs(blocks)
        ]
    )
    return updated, arrow_block - arrow_total


def exchange_kernel(
    supers, cols, fanout,
    parent_ref, off_hbm, inv_ref, arrow_rows_hbm, target_hbm, arrow_block_hbm,
    updated_ref, arrow_ref,
    off_ref, arrow_rows_ref, target_ref, arrow_block_ref,
    inv_all, outgoing, off_all, panel, sums, landed, arrow_all, total,
    inv_send, inv_recv, off_send, off_recv, sum_send, sum_recv,
    arrow_send, arrow_recv, cast_send, cast_recv, load_sem,
):
    sources = inv_ref.shape[0]
    slab = inv_ref.shape[1]
    width = inv_ref.shape[2]
    blocks = width // BLK
    pairs = block_pairs(blocks)
    rounds = supers // cols
    me_s, me_c = lax.axis_index("super"), lax.axis_index("col")
    y, core = lax.div(me_c, 2), lax.rem(me_c, 2)
    beside = 2 * y + 1 - core
    across = 2 * (1 - y) + core
    diagonal = 2 * (1 - y) + 1 - core
    peers = (beside, across, diagonal)

    loads = [
        pltpu.make_async_copy(src, dst, load_sem.at[n])
        for n, (src, dst) in enumerate(
            (
                (off_hbm, off_ref),
                (inv_ref, inv_all.at[:, me_c]),
                (arrow_rows_hbm, arrow_rows_ref),
                (target_hbm, target_ref),
                (arrow_block_hbm, arrow_block_ref),
            )
        )
    ]
    for load in loads:
        load.start()

    barrier = pltpu.get_barrier_semaphore()
    for peer in peers:
        pl.semaphore_signal(
            barrier, inc=1, device_id={"super": me_s, "col": peer}, device_id_type=MESH
        )
    for d in range(1, supers):
        pl.semaphore_signal(
            barrier,
            inc=1,
            device_id={"super": lax.rem(me_s + d, supers), "col": me_c},
            device_id_type=MESH,
        )
    pl.semaphore_wait(barrier, cols - 1 + supers - 1)

    def remote(src, dst, send, recv, sup, col):
        return pltpu.make_async_remote_copy(
            src_ref=src,
            dst_ref=dst,
            send_sem=send,
            recv_sem=recv,
            device_id={"super": sup, "col": col},
            device_id_type=MESH,
        )

    inv_across = remote(inv_ref, inv_all.at[:, me_c], inv_send.at[1], inv_recv.at[1], me_s, across)
    inv_across.start()
    inv_beside = remote(inv_ref, inv_all.at[:, me_c], inv_send.at[0], inv_recv.at[0], me_s, beside)
    inv_beside.start()

    entries = [
        (parent_ref[j, t], j * fanout + t, j) for j in range(sources) for t in range(fanout)
    ]
    half = lax.div(me_s, cols)

    def parent_of(col, t):
        return col + cols * lax.rem(half + 1 + t, rounds)

    def items(col, t):
        p = parent_of(col, t)
        first, first_source = jnp.int32(len(entries) - 1), jnp.int32(sources - 1)
        second, second_source = jnp.int32(0), jnp.int32(0)
        for owner, item, source in entries:
            hit = owner == p
            first = jnp.where(hit, jnp.minimum(first, item), first)
            first_source = jnp.where(hit, jnp.minimum(first_source, source), first_source)
            second = jnp.where(hit, item, second)
            second_source = jnp.where(hit, source, second_source)
        return (first, second), (first_source, second_source)

    loads[0].wait()
    off_copies = {}
    own_sources = []
    for t in range(rounds):
        for k in (1, 2, 0):
            chosen, _ = items(peers[k], t)
            for m in range(2):
                outgoing[k, t, m] = off_ref[chosen[m]]
            copy = remote(
                outgoing.at[k, t],
                off_all.at[t, :, me_c],
                off_send.at[k, t],
                off_recv.at[k, t],
                me_s,
                peers[k],
            )
            copy.start()
            off_copies[k, t] = copy
        chosen, chosen_sources = items(me_c, t)
        own_sources.append(chosen_sources)
        for m in range(2):
            off_all[t, m, me_c] = off_ref[chosen[m]]
    for load in loads[1:]:
        load.wait()

    inv_across.wait_recv()
    inv_onward = remote(
        inv_all.at[:, across], inv_all.at[:, across], inv_send.at[2], inv_recv.at[2], me_s, beside
    )
    inv_onward.start()
    inv_beside.wait_recv()
    inv_onward.wait_recv()

    nt = (((1,), (1,)), ((), ()))
    arrow_sum = jnp.zeros(arrow_ref.shape, jnp.float32)
    for j in range(sources):
        rows = lax.dot_general(
            arrow_rows_ref[j],
            inv_all[j].reshape(width, width),
            nt,
            preferred_element_type=jnp.float32,
        ).astype(jnp.bfloat16)
        arrow_sum = arrow_sum + lax.dot_general(
            rows, rows, nt, preferred_element_type=jnp.float32
        )
    arrow_all[me_s] = arrow_sum
    arrow_copies = []
    for d in range(1, supers):
        copy = remote(
            arrow_all.at[me_s],
            arrow_all.at[me_s],
            arrow_send.at[d],
            arrow_recv.at[d],
            lax.rem(me_s + d, supers),
            me_c,
        )
        copy.start()
        arrow_copies.append(copy)

    def part(r):
        return slice(pairs.index((r, r)), pairs.index((r, blocks - 1)) + 1)

    def sum_copy(t, r, slot, sup, col):
        here = pl.ds(part(r).start, part(r).stop - part(r).start)
        return remote(
            sums.at[t, here], landed.at[slot, here], sum_send.at[t, r], sum_recv.at[slot, r], sup, col
        )

    for t in range(rounds):
        for k in range(3):
            off_copies[k, t].wait_recv()
        for m in range(2):
            panel[:, m * width : (m + 1) * width] = lax.dot_general(
                off_all[t, m].reshape(width, width),
                inv_all[own_sources[t][m]].reshape(width, width),
                nt,
                preferred_element_type=jnp.float32,
            ).astype(jnp.bfloat16)
        p = parent_of(me_c, t)
        for r in range(blocks):
            product = lax.dot_general(
                panel[r * BLK : (r + 1) * BLK, :],
                panel[r * BLK :, :],
                nt,
                preferred_element_type=jnp.float32,
            ).astype(jnp.bfloat16)
            for c in range(r, blocks):
                sums[t, pairs.index((r, c))] = product[:, (c - r) * BLK : (c - r + 1) * BLK]

            @pl.when(p != me_s)
            def _():
                sum_copy(t, r, me_s, p, me_c).start()

            @pl.when(p == me_s)
            def _():
                landed[me_s, part(r)] = sums[t, part(r)]

    chief = lax.rem(me_s, cols)

    def cast(n, r, col):
        return remote(
            total.at[pl.ds(part(r).start, blocks - r)], total.at[pl.ds(part(r).start, blocks - r)], cast_send.at[n, r], cast_recv.at[r], me_s, col
        )

    @pl.when(me_c == chief)
    def _():
        for r in range(blocks):
            for d in range(1, supers):
                sum_copy(0, r, lax.rem(me_s + d, supers), me_s, beside).wait_recv()
            for b in range(part(r).start, part(r).stop):
                acc = landed[0, b].astype(jnp.float32)
                for s in range(1, supers):
                    acc = acc + landed[s, b].astype(jnp.float32)
                total[b] = acc.astype(jnp.bfloat16)
            cast(0, r, across).start()
            cast(1, r, beside).start()
        for r in range(blocks):
            cast(0, r, across).wait_send()
            cast(1, r, beside).wait_send()

    @pl.when(me_c != chief)
    def _():
        for r in range(blocks):
            cast(0, r, beside).wait_recv()

            @pl.when(across == chief)
            def _():
                cast(1, r, beside).start()

    @pl.when(across == chief)
    def _():
        for r in range(blocks):
            cast(1, r, beside).wait_send()

    for n, (r, c) in enumerate(pairs):
        updated_ref[n] = target_ref[
            0, r * BLK : (r + 1) * BLK, c * BLK : (c + 1) * BLK
        ] - total[n].astype(jnp.float32)

    for copy in arrow_copies:
        copy.wait_recv()
    arrow_total = arrow_all[0]
    for s in range(1, supers):
        arrow_total = arrow_total + arrow_all[s]
    arrow_ref[...] = arrow_block_ref[...] - arrow_total

    for copy in (inv_across, inv_beside, inv_onward, *off_copies.values(), *arrow_copies):
        copy.wait_send()
    for t in range(rounds):
        p = parent_of(me_c, t)

        @pl.when(p != me_s)
        def _():
            for r in range(blocks):
                sum_copy(t, r, me_s, p, me_c).wait_send()


def exchanged(parent, off_blocks, inv_factors, arrow_rows, target_blocks, arrow_block):
    supers, cols = lax.axis_size("super"), lax.axis_size("col")
    sources, fanout, slab, width = off_blocks.shape
    arrow = arrow_block.shape[0]
    rounds = supers // cols
    count = len(block_pairs(width // BLK))
    vmem = pl.BlockSpec(memory_space=pltpu.VMEM)
    hbm = pl.BlockSpec(memory_space=pltpu.HBM)
    bf16, f32 = jnp.bfloat16, jnp.float32
    dma = pltpu.SemaphoreType.DMA
    return pl.pallas_call(
        functools.partial(exchange_kernel, supers, cols, fanout),
        out_shape=(
            jax.ShapeDtypeStruct((count, BLK, BLK), f32),
            jax.ShapeDtypeStruct((arrow, arrow), f32),
        ),
        in_specs=[pl.BlockSpec(memory_space=pltpu.SMEM)] + [hbm] * 5,
        out_specs=(vmem, vmem),
        scratch_shapes=[
            pltpu.VMEM((sources * fanout, slab, width), bf16),
            pltpu.VMEM((sources, arrow, width), bf16),
            pltpu.VMEM((1, width, width), f32),
            pltpu.VMEM((arrow, arrow), f32),
            pltpu.VMEM((sources, cols, slab, width), bf16),
            pltpu.VMEM((cols - 1, rounds, 2, slab, width), bf16),
            pltpu.VMEM((rounds, 2, cols, slab, width), bf16),
            pltpu.VMEM((width, 2 * width), bf16),
            pltpu.VMEM((rounds, count, BLK, BLK), bf16),
            pltpu.VMEM((supers, count, BLK, BLK), bf16),
            pltpu.VMEM((supers, arrow, arrow), f32),
            pltpu.VMEM((count, BLK, BLK), bf16),
            dma((3,)),
            dma((3,)),
            dma((3, rounds)),
            dma((3, rounds)),
            dma((rounds, width // BLK)),
            dma((supers, width // BLK)),
            dma((supers,)),
            dma((supers,)),
            dma((2, width // BLK)),
            dma((width // BLK,)),
            dma((5,)),
        ],
        compiler_params=pltpu.CompilerParams(
            collective_id=0, has_side_effects=True, vmem_limit_bytes=40 * 2**20
        ),
        name="exchange",
    )(
        parent,
        off_blocks.reshape(sources * fanout, slab, width),
        inv_factors,
        arrow_rows,
        target_blocks,
        arrow_block,
    )


def shards(parent, off_blocks, inv_factors, arrow_rows, target_blocks, arrow_block):
    supers, cols = lax.axis_size("super"), lax.axis_size("col")
    entries = off_blocks.shape[0] * off_blocks.shape[1]
    form = exchanged if cols == 4 and supers == 2 * cols and entries == 2 * supers else routed
    updated, arrow_update = form(
        parent, off_blocks, inv_factors, arrow_rows, target_blocks, arrow_block
    )
    return factor_rows(updated, target_blocks.shape[1]), arrow_update


def solution(mesh):
    placed = (
        P("super", None),
        P("super", None, "col", None),
        P("super", "col", None),
        P("super", None, None),
        P("super", None, None),
        P(),
    )
    return jax.shard_map(
        shards,
        mesh=mesh,
        in_specs=placed,
        out_specs=(P("super", "col", None), P()),
        check_vma=False,
    )
```

```python
import functools

import jax
import jax.numpy as jnp
from jax import lax
from jax.experimental import pallas as pl
from jax.experimental.pallas import tpu as pltpu
from jax.sharding import PartitionSpec as P

MESH = pl.DeviceIdType.MESH
EXACT = lax.Precision.HIGHEST
BLK = 128
SUB = 16


def block_pairs(blocks):
    return [(r, c) for r in range(blocks) for c in range(r, blocks)]


def halves(x):
    high = x.astype(jnp.bfloat16)
    return high, (x - high.astype(jnp.float32)).astype(jnp.bfloat16)


def thin_product(a, b):
    a_high, a_low = halves(a)
    b_high, b_low = halves(b)
    return lax.dot_general(
        jnp.concatenate([a_high, a_high, a_low], axis=0),
        jnp.concatenate([b_high, b_low, b_high], axis=0),
        (((0,), (0,)), ((), ())),
        preferred_element_type=jnp.float32,
    )


def eliminate(rows, extra, step):
    row_ids = lax.broadcasted_iota(jnp.int32, (SUB, BLK), 0)
    base = step * SUB
    cols = [
        jnp.broadcast_to(rows[:, base + b : base + b + 1], (SUB, BLK)) for b in range(SUB)
    ]
    scale = jnp.zeros((SUB, BLK), jnp.float32)
    for m in range(SUB):
        pivot = jnp.broadcast_to(cols[m][m : m + 1], (SUB, BLK))
        inv = lax.rsqrt(pivot)
        scale = jnp.where(row_ids == m, inv, scale)
        if m == SUB - 1:
            break
        low = cols[m] * inv
        for b in range(m + 1, SUB):
            cols[b] = cols[b] - low * jnp.broadcast_to(low[b : b + 1], (SUB, BLK))
        low = jnp.where(row_ids > m, low * inv, 0.0)
        rows = rows - low * jnp.broadcast_to(rows[m : m + 1], (SUB, BLK))
        if extra is not None:
            extra = extra - low * jnp.broadcast_to(extra[m : m + 1], (SUB, BLK))
    return rows * scale, None if extra is None else extra * scale


def cholesky_kernel(updated_ref, out_ref, u_ref, d_ref, q_ref):
    blocks = out_ref.shape[2] // BLK
    pairs = block_pairs(blocks)
    row_ids = lax.broadcasted_iota(jnp.int32, (BLK, BLK), 0)
    col_ids = lax.broadcasted_iota(jnp.int32, (BLK, BLK), 1)
    for kb in range(blocks):
        lo = kb * BLK
        update = None
        if kb:
            update = lax.dot_general(
                u_ref[0:lo, lo : lo + BLK],
                u_ref[0:lo, lo:],
                (((0,), (0,)), ((), ())),
                precision=EXACT,
                preferred_element_type=jnp.float32,
            )
        panel = []
        for cb in range(kb, blocks):
            part = updated_ref[pairs.index((kb, cb))]
            if kb:
                part = part - update[:, (cb - kb) * BLK : (cb - kb + 1) * BLK]
            panel.append(part)
        last = kb == blocks - 1
        d_ref[...] = panel[0]
        if not last:
            q_ref[...] = (row_ids == col_ids).astype(jnp.float32)
        steps = BLK // SUB
        for step in range(steps):
            here = slice(step * SUB, (step + 1) * SUB)
            rows, extra = eliminate(d_ref[here], None if last else q_ref[here], step)
            d_ref[here] = rows
            if not last:
                q_ref[here] = extra
            if step < steps - 1:
                below = slice((step + 1) * SUB, BLK)
                right = rows if last else jnp.concatenate([rows, extra], axis=1)
                change = thin_product(rows, right)
                d_ref[below] = d_ref[below] - change[below, :BLK]
                if not last:
                    q_ref[below] = q_ref[below] - change[below, BLK:]
        u_ref[lo : lo + BLK, lo : lo + BLK] = jnp.where(row_ids <= col_ids, d_ref[...], 0.0)
        if not last:
            u_ref[lo : lo + BLK, lo + BLK :] = jnp.dot(
                q_ref[...],
                jnp.concatenate(panel[1:], axis=1),
                precision=EXACT,
                preferred_element_type=jnp.float32,
            )
    me = lax.axis_index("col")
    for mine in range(blocks):

        @pl.when(me == mine)
        def _():
            for b in range(blocks):
                there = slice(b * BLK, (b + 1) * BLK)
                if b <= mine:
                    out_ref[0, :, there] = u_ref[there, mine * BLK : (mine + 1) * BLK].T
                else:
                    out_ref[0, :, there] = jnp.zeros((BLK, BLK), jnp.float32)


def factor_rows(updated, width):
    vmem = pl.BlockSpec(memory_space=pltpu.VMEM)
    return pl.pallas_call(
        cholesky_kernel,
        out_shape=jax.ShapeDtypeStruct((1, BLK, width), jnp.float32),
        in_specs=[vmem],
        out_specs=vmem,
        scratch_shapes=[
            pltpu.VMEM((width, width), jnp.float32),
            pltpu.VMEM((BLK, BLK), jnp.float32),
            pltpu.VMEM((BLK, BLK), jnp.float32),
        ],
        compiler_params=pltpu.CompilerParams(vmem_limit_bytes=24 * 2**20),
        name="factor",
    )(updated)

def routed(parent, off_blocks, inv_factors, arrow_rows, target_blocks, arrow_block):
    supers = lax.axis_size("super")
    sources, fanout, slab_rows, block_width = off_blocks.shape
    item_count = sources * fanout
    capacity = max(2, (item_count + supers - 1) // supers)
    stacked_rows = off_blocks.reshape(sources, fanout * slab_rows, block_width)
    portion = lax.all_gather(inv_factors, "col", axis=1, tiled=True)
    rows_part = jnp.einsum(
        "jrk,jck->jrc", stacked_rows, portion, preferred_element_type=jnp.float32
    ).astype(jnp.bfloat16)
    arrow_panels = jnp.einsum(
        "jak,jck->jac", arrow_rows, portion, preferred_element_type=jnp.float32
    ).astype(jnp.bfloat16)
    arrow_local = jnp.einsum(
        "jac,jbc->ab", arrow_panels, arrow_panels, preferred_element_type=jnp.float32
    )
    arrow_total = lax.psum(arrow_local, "super")
    row_panels = rows_part.reshape(sources, fanout, slab_rows, block_width)
    panels = lax.all_to_all(row_panels, "col", split_axis=3, concat_axis=2, tiled=True)
    column_panels = panels.reshape(item_count, block_width, panels.shape[3])
    owners = parent.reshape(item_count)
    item_index = jnp.arange(item_count, dtype=jnp.int32)
    matching = owners[:, None] == owners[None, :]
    earlier = item_index[None, :] < item_index[:, None]
    position = jnp.sum((matching & earlier).astype(jnp.int32), axis=1)
    target_slot = owners * capacity + position
    slots = jnp.arange(supers * capacity, dtype=jnp.int32)
    chosen = (slots[:, None] == target_slot[None, :]).astype(jnp.bfloat16)
    packed = jnp.einsum(
        "pi,irc->prc", chosen, column_panels, preferred_element_type=jnp.float32
    ).astype(jnp.bfloat16)
    packed = packed.reshape(supers, capacity, block_width, column_panels.shape[2])
    received = lax.all_to_all(packed, "super", split_axis=0, concat_axis=0, tiled=True)
    schur_local = jnp.einsum(
        "dmrc,dmsc->rs", received, received, preferred_element_type=jnp.float32
    )
    schur = lax.psum(schur_local.astype(jnp.bfloat16), "col")
    blocks = block_width // BLK
    whole = target_blocks[0] - schur.astype(jnp.float32)
    updated = jnp.stack(
        [
            whole[r * BLK : (r + 1) * BLK, c * BLK : (c + 1) * BLK]
            for r, c in block_pairs(blocks)
        ]
    )
    return updated, arrow_block - arrow_total


def exchange_kernel(
    supers, cols, fanout,
    parent_ref, off_hbm, inv_ref, arrow_rows_hbm, target_hbm, arrow_block_hbm,
    updated_ref, arrow_ref,
    off_ref, arrow_rows_ref, target_ref, arrow_block_ref,
    inv_all, outgoing, off_all, panel, sums, landed, arrow_all, total,
    inv_send, inv_recv, off_send, off_recv, sum_send, sum_recv,
    arrow_send, arrow_recv, cast_send, cast_recv, load_sem,
):
    sources = inv_ref.shape[0]
    slab = inv_ref.shape[1]
    width = inv_ref.shape[2]
    blocks = width // BLK
    pairs = block_pairs(blocks)
    rounds = supers // cols
    me_s, me_c = lax.axis_index("super"), lax.axis_index("col")
    y, core = lax.div(me_c, 2), lax.rem(me_c, 2)
    beside = 2 * y + 1 - core
    across = 2 * (1 - y) + core
    diagonal = 2 * (1 - y) + 1 - core
    peers = (beside, across, diagonal)

    loads = [
        pltpu.make_async_copy(src, dst, load_sem.at[n])
        for n, (src, dst) in enumerate(
            (
                (off_hbm, off_ref),
                (inv_ref, inv_all.at[:, me_c]),
                (arrow_rows_hbm, arrow_rows_ref),
                (target_hbm, target_ref),
                (arrow_block_hbm, arrow_block_ref),
            )
        )
    ]
    for load in loads:
        load.start()

    barrier = pltpu.get_barrier_semaphore()
    for peer in peers:
        pl.semaphore_signal(
            barrier, inc=1, device_id={"super": me_s, "col": peer}, device_id_type=MESH
        )
    for d in range(1, supers):
        pl.semaphore_signal(
            barrier,
            inc=1,
            device_id={"super": lax.rem(me_s + d, supers), "col": me_c},
            device_id_type=MESH,
        )
    pl.semaphore_wait(barrier, cols - 1 + supers - 1)

    def remote(src, dst, send, recv, sup, col):
        return pltpu.make_async_remote_copy(
            src_ref=src,
            dst_ref=dst,
            send_sem=send,
            recv_sem=recv,
            device_id={"super": sup, "col": col},
            device_id_type=MESH,
        )

    inv_across = remote(inv_ref, inv_all.at[:, me_c], inv_send.at[1], inv_recv.at[1], me_s, across)
    inv_across.start()
    inv_beside = remote(inv_ref, inv_all.at[:, me_c], inv_send.at[0], inv_recv.at[0], me_s, beside)
    inv_beside.start()

    entries = [
        (parent_ref[j, t], j * fanout + t, j) for j in range(sources) for t in range(fanout)
    ]
    half = lax.div(me_s, cols)

    def parent_of(col, t):
        return col + cols * lax.rem(half + 1 + t, rounds)

    def items(col, t):
        p = parent_of(col, t)
        first, first_source = jnp.int32(len(entries) - 1), jnp.int32(sources - 1)
        second, second_source = jnp.int32(0), jnp.int32(0)
        for owner, item, source in entries:
            hit = owner == p
            first = jnp.where(hit, jnp.minimum(first, item), first)
            first_source = jnp.where(hit, jnp.minimum(first_source, source), first_source)
            second = jnp.where(hit, item, second)
            second_source = jnp.where(hit, source, second_source)
        return (first, second), (first_source, second_source)

    loads[0].wait()
    off_copies = {}
    own_sources = []
    for t in range(rounds):
        for k in (1, 2, 0):
            chosen, _ = items(peers[k], t)
            for m in range(2):
                outgoing[k, t, m] = off_ref[chosen[m]]
            copy = remote(
                outgoing.at[k, t],
                off_all.at[t, :, me_c],
                off_send.at[k, t],
                off_recv.at[k, t],
                me_s,
                peers[k],
            )
            copy.start()
            off_copies[k, t] = copy
        chosen, chosen_sources = items(me_c, t)
        own_sources.append(chosen_sources)
        for m in range(2):
            off_all[t, m, me_c] = off_ref[chosen[m]]
    for load in loads[1:]:
        load.wait()

    inv_across.wait_recv()
    inv_onward = remote(
        inv_all.at[:, across], inv_all.at[:, across], inv_send.at[2], inv_recv.at[2], me_s, beside
    )
    inv_onward.start()
    inv_beside.wait_recv()
    inv_onward.wait_recv()

    nt = (((1,), (1,)), ((), ()))
    arrow_sum = jnp.zeros(arrow_ref.shape, jnp.float32)
    for j in range(sources):
        rows = lax.dot_general(
            arrow_rows_ref[j],
            inv_all[j].reshape(width, width),
            nt,
            preferred_element_type=jnp.float32,
        ).astype(jnp.bfloat16)
        arrow_sum = arrow_sum + lax.dot_general(
            rows, rows, nt, preferred_element_type=jnp.float32
        )
    arrow_all[me_s] = arrow_sum
    arrow_copies = []
    for d in range(1, supers):
        copy = remote(
            arrow_all.at[me_s],
            arrow_all.at[me_s],
            arrow_send.at[d],
            arrow_recv.at[d],
            lax.rem(me_s + d, supers),
            me_c,
        )
        copy.start()
        arrow_copies.append(copy)

    def part(r):
        return slice(pairs.index((r, r)), pairs.index((r, blocks - 1)) + 1)

    def sum_copy(t, r, slot, sup, col):
        here = pl.ds(part(r).start, part(r).stop - part(r).start)
        return remote(
            sums.at[t, here], landed.at[slot, here], sum_send.at[t, r], sum_recv.at[slot, r], sup, col
        )

    for t in range(rounds):
        for k in range(3):
            off_copies[k, t].wait_recv()
        for m in range(2):
            panel[:, m * width : (m + 1) * width] = lax.dot_general(
                off_all[t, m].reshape(width, width),
                inv_all[own_sources[t][m]].reshape(width, width),
                nt,
                preferred_element_type=jnp.float32,
            ).astype(jnp.bfloat16)
        p = parent_of(me_c, t)
        for r in range(blocks):
            product = lax.dot_general(
                panel[r * BLK : (r + 1) * BLK, :],
                panel[r * BLK :, :],
                nt,
                preferred_element_type=jnp.float32,
            ).astype(jnp.bfloat16)
            for c in range(r, blocks):
                sums[t, pairs.index((r, c))] = product[:, (c - r) * BLK : (c - r + 1) * BLK]

            @pl.when(p != me_s)
            def _():
                sum_copy(t, r, me_s, p, me_c).start()

            @pl.when(p == me_s)
            def _():
                landed[me_s, part(r)] = sums[t, part(r)]

    chief = lax.rem(me_s, cols)

    def cast(n, r, col):
        return remote(
            total.at[pl.ds(part(r).start, blocks - r)], total.at[pl.ds(part(r).start, blocks - r)], cast_send.at[n, r], cast_recv.at[r], me_s, col
        )

    @pl.when(me_c == chief)
    def _():
        for r in range(blocks):
            for d in range(1, supers):
                sum_copy(0, r, lax.rem(me_s + d, supers), me_s, beside).wait_recv()
            for b in range(part(r).start, part(r).stop):
                acc = landed[0, b].astype(jnp.float32)
                for s in range(1, supers):
                    acc = acc + landed[s, b].astype(jnp.float32)
                total[b] = acc.astype(jnp.bfloat16)
            cast(0, r, across).start()
            cast(1, r, beside).start()
        for r in range(blocks):
            cast(0, r, across).wait_send()
            cast(1, r, beside).wait_send()

    @pl.when(me_c != chief)
    def _():
        for r in range(blocks):
            cast(0, r, beside).wait_recv()

            @pl.when(across == chief)
            def _():
                cast(1, r, beside).start()

    @pl.when(across == chief)
    def _():
        for r in range(blocks):
            cast(1, r, beside).wait_send()

    for n, (r, c) in enumerate(pairs):
        updated_ref[n] = target_ref[
            0, r * BLK : (r + 1) * BLK, c * BLK : (c + 1) * BLK
        ] - total[n].astype(jnp.float32)

    for copy in arrow_copies:
        copy.wait_recv()
    arrow_total = arrow_all[0]
    for s in range(1, supers):
        arrow_total = arrow_total + arrow_all[s]
    arrow_ref[...] = arrow_block_ref[...] - arrow_total

    for copy in (inv_across, inv_beside, inv_onward, *off_copies.values(), *arrow_copies):
        copy.wait_send()
    for t in range(rounds):
        p = parent_of(me_c, t)

        @pl.when(p != me_s)
        def _():
            for r in range(blocks):
                sum_copy(t, r, me_s, p, me_c).wait_send()


def exchanged(parent, off_blocks, inv_factors, arrow_rows, target_blocks, arrow_block):
    supers, cols = lax.axis_size("super"), lax.axis_size("col")
    sources, fanout, slab, width = off_blocks.shape
    arrow = arrow_block.shape[0]
    rounds = supers // cols
    count = len(block_pairs(width // BLK))
    vmem = pl.BlockSpec(memory_space=pltpu.VMEM)
    hbm = pl.BlockSpec(memory_space=pltpu.HBM)
    bf16, f32 = jnp.bfloat16, jnp.float32
    dma = pltpu.SemaphoreType.DMA
    return pl.pallas_call(
        functools.partial(exchange_kernel, supers, cols, fanout),
        out_shape=(
            jax.ShapeDtypeStruct((count, BLK, BLK), f32),
            jax.ShapeDtypeStruct((arrow, arrow), f32),
        ),
        in_specs=[pl.BlockSpec(memory_space=pltpu.SMEM)] + [hbm] * 5,
        out_specs=(vmem, vmem),
        scratch_shapes=[
            pltpu.VMEM((sources * fanout, slab, width), bf16),
            pltpu.VMEM((sources, arrow, width), bf16),
            pltpu.VMEM((1, width, width), f32),
            pltpu.VMEM((arrow, arrow), f32),
            pltpu.VMEM((sources, cols, slab, width), bf16),
            pltpu.VMEM((cols - 1, rounds, 2, slab, width), bf16),
            pltpu.VMEM((rounds, 2, cols, slab, width), bf16),
            pltpu.VMEM((width, 2 * width), bf16),
            pltpu.VMEM((rounds, count, BLK, BLK), bf16),
            pltpu.VMEM((supers, count, BLK, BLK), bf16),
            pltpu.VMEM((supers, arrow, arrow), f32),
            pltpu.VMEM((count, BLK, BLK), bf16),
            dma((3,)),
            dma((3,)),
            dma((3, rounds)),
            dma((3, rounds)),
            dma((rounds, width // BLK)),
            dma((supers, width // BLK)),
            dma((supers,)),
            dma((supers,)),
            dma((2, width // BLK)),
            dma((width // BLK,)),
            dma((5,)),
        ],
        compiler_params=pltpu.CompilerParams(
            collective_id=0, has_side_effects=True, vmem_limit_bytes=65408 * 2**10
        ),
        name="exchange",
    )(
        parent,
        off_blocks.reshape(sources * fanout, slab, width),
        inv_factors,
        arrow_rows,
        target_blocks,
        arrow_block,
    )


def shards(parent, off_blocks, inv_factors, arrow_rows, target_blocks, arrow_block):
    supers, cols = lax.axis_size("super"), lax.axis_size("col")
    entries = off_blocks.shape[0] * off_blocks.shape[1]
    form = exchanged if cols == 4 and supers == 2 * cols and entries == 2 * supers else routed
    updated, arrow_update = form(
        parent, off_blocks, inv_factors, arrow_rows, target_blocks, arrow_block
    )
    return factor_rows(updated, target_blocks.shape[1]), arrow_update


def solution(mesh):
    placed = (
        P("super", None),
        P("super", None, "col", None),
        P("super", "col", None),
        P("super", None, None),
        P("super", None, None),
        P(),
    )
    return jax.shard_map(
        shards,
        mesh=mesh,
        in_specs=placed,
        out_specs=(P("super", "col", None), P()),
        check_vma=False,
    )
```
